32 devices in a mesh: lon: 8 (over z, core), lat: 4 (over y, x).
Axes of the slice: x: 2, y: 2, z: 4, core: 2. Of those that a mesh axis runs over, the one named last changes fastest.
Arguments:
- zonal_velocity: float32 [75, 96, 3072], P(None, 'lat', 'lon'), may hold values from -6 to 6
- meridional_velocity: float32 [75, 96, 3072], P(None, 'lat', 'lon'), may hold values from -6 to 6
- tracer: float32 [75, 96, 3072], P(None, 'lat', 'lon'), may hold values from -6 to 6
- land_mask: int32 [96, 3072], P('lat', 'lon'), may hold values 0 or 1
- remap_bounds: int32 [8, 256, 31], P('lat', 'lon'), may hold values from 0 to 75, as said below
- nest_owner: int32 [8, 256], P('lat', 'lon'), may hold values from 0 to 8, as said below
Outputs:
- zonal_new: float32 [75, 96, 3072], P(None, 'lat', 'lon')
- meridional_new: float32 [75, 96, 3072], P(None, 'lat', 'lon')
- tracer_new: float32 [75, 96, 3072], P(None, 'lat', 'lon')
- nest_tiles: float32 [4, 8, 16, 30, 1296], P('lat', 'lon')
The draws below stay inside these ranges and needn't reach their ends.
Inputs may be any that keep to these rules, and one draw needn't show every extreme that they name: `remap_bounds`: for each parent block the 31 entries rise strictly from 0 and the last lies between 30 and 75. `nest_owner`: A value below 8 puts the block in the nest, owned by the tile at that longitude index in the block's own latitude band; 8 marks a block outside the nest. Among the blocks of one tile at most 2 share an owner, and at most 16 lie in the nest.
All inputs are finite; a program needn't handle non-finite values. No bound on the sum of `land_mask` on one device may be relied on, other than what follows from the above.
Results may differ from the reference program's by a relative error of at most 0.0003.
Values sent between devices are 32-bit elements; how exact they have to be, the bound alone decides.
A program may use at most 192 MiB of HBM per device.

```python
import math
import jax
import jax.numpy as jnp
import numpy as np
from jax import lax

LEVELS = 75
SIGMA = 30
TILE = 12
CAP = 2
BLK_X = 32
BLK_Y = 2
CELLS_Y = 24
NX = 3072
NY = 96
NBX = 256
NBY = 8
SLOTS = 16
RIM = 256
NCELL = 1296
N_LON = 8
N_LAT = 4


def draw_remap_bounds(key, part):
    first_key, second_key, row_key, col_key = jax.random.split(key, 4)
    half_count = SIGMA // 2
    upper_extra = jax.random.randint(first_key, (NBY, NBX, half_count), 0, 3)
    lower_extra = jax.random.randint(second_key, (NBY, NBX, SIGMA - half_count), 0, 2)
    extra = jnp.concatenate([upper_extra, lower_extra], axis=-1)
    fullest = jnp.concatenate([jnp.full((half_count,), 2, jnp.int32), jnp.full((SIGMA - half_count,), 1, jnp.int32)])
    pick_row = jax.random.randint(row_key, (), 0, NBY)
    pick_col = jax.random.randint(col_key, (), 0, NBX)
    chosen = (jnp.arange(NBY)[:, None] == pick_row) & (jnp.arange(NBX)[None, :] == pick_col)
    extra = jnp.where(chosen[..., None], fullest[None, None, :], extra)
    counts = 1 + extra
    edge_list = jnp.concatenate([jnp.zeros((NBY, NBX, 1), jnp.int32), jnp.cumsum(counts, axis=-1)], axis=-1)
    return edge_list.astype(jnp.int32)


def draw_nest_owner(key, part):
    per_dev = BLK_Y * BLK_X
    nest_most = min(per_dev // 4, CAP * N_LON)
    spare_count = nest_most - CAP

    def one_band(band_index):
        band_key = jax.random.fold_in(key, band_index)
        busiest = jax.random.randint(jax.random.fold_in(band_key, 7), (), 0, N_LON)
        fullest = jax.random.randint(jax.random.fold_in(band_key, 11), (), 0, N_LON)

        def one_dev(lon_index):
            dev_key = jax.random.fold_in(band_key, 100 + lon_index)
            dev_keys = jax.random.split(dev_key, 2 + CAP)
            middle = 2 + jax.random.permutation(dev_keys[0], per_dev - 2)
            ranking = jnp.concatenate([jnp.zeros((1,), middle.dtype), middle, jnp.ones((1,), middle.dtype)])
            others_count = jax.random.randint(dev_keys[1], (), spare_count // 2, spare_count + 1)
            others_count = jnp.where(lon_index == fullest, spare_count, others_count)
            others = jnp.concatenate([jax.random.permutation(dev_keys[2 + c], N_LON - 1) for c in range(CAP)])
            others = others + (others >= busiest).astype(others.dtype)
            picked = others[jnp.clip(ranking - CAP, 0, CAP * (N_LON - 1) - 1)]
            owners = jnp.where(ranking < CAP, busiest, jnp.where(ranking < CAP + others_count, picked, N_LON))
            return owners.reshape(BLK_Y, BLK_X).astype(jnp.int32)
        return jax.vmap(one_dev)(jnp.arange(N_LON, dtype=jnp.int32))
    owner_grid = jax.vmap(one_band)(jnp.arange(N_LAT, dtype=jnp.int32))
    return owner_grid.transpose(0, 2, 1, 3).reshape(NBY, NBX).astype(jnp.int32)


def plant(array, stream_key, smallest, high):
    extent = array.shape
    place = [jax.random.randint(jax.random.fold_in(stream_key, axis), (), 0, extent[axis]) for axis in range(len(extent))]
    array = array.at[tuple(place)].set(smallest)
    longest = extent.index(max(extent))
    place[longest] = (place[longest] + 1) % extent[longest]
    return array.at[tuple(place)].set(high)


def levels(own_key, extent, cuts, smallest, high):
    factor_of, own = 1.0, jax.random.fold_in(own_key, 6)
    for dim, parts in cuts:
        draws = jnp.exp(jax.random.uniform(jax.random.fold_in(own, dim), (parts,), jnp.float32, smallest / len(cuts), high / len(cuts)))
        factor_of = factor_of * jnp.repeat(draws, extent[dim] // parts).reshape([-1 if axis == dim else 1 for axis in range(len(extent))])
    return factor_of


def scatter_about(key, shape, width, most, cuts=(), kind=jnp.bfloat16):
    level = levels(key, shape, cuts, -0.22, 0.18) if cuts else 1.0
    array = jax.random.normal(key, shape, jnp.float32) * width * level
    return jnp.minimum(jnp.maximum(array, -most), most).astype(kind)


def setup_inputs(seed: int = 0) -> dict:
    arg_keys = jax.random.split(jax.random.key(seed), 7)
    return {
        "zonal_velocity": scatter_about(arg_keys[0], (LEVELS, NY, NX), 1.0, 6.0, ((1, 4), (2, 8)), jnp.float32),
        "meridional_velocity": scatter_about(arg_keys[1], (LEVELS, NY, NX), 1.0, 6.0, ((1, 4), (2, 8)), jnp.float32),
        "tracer": scatter_about(arg_keys[2], (LEVELS, NY, NX), 1.0, 6.0, ((1, 4), (2, 8)), jnp.float32),
        "land_mask": plant((jax.random.randint(arg_keys[3], (NY, NX), 0, 4) < 3).astype(jnp.int32), jax.random.fold_in(arg_keys[3], 1), 0, 1),
        "remap_bounds": draw_remap_bounds(jax.random.fold_in(arg_keys[6], 71), 0),
        "nest_owner": draw_nest_owner(jax.random.fold_in(arg_keys[6], 71), 0),
    }


ADVECT = 0.25
DIFFUSE = 0.15
PRESSURE = 0.3
ROTATION = 0.6
BASE_LATITUDE = 20.0
ROW_DEGREES = 1.0 / 12.0


def cubic_weights(tile_cells):
    span_len = tile_cells + 4
    weights = np.zeros((span_len, 3 * tile_cells), np.float32)
    for cell_idx in range(tile_cells):
        for phase_idx in range(3):
            if phase_idx == 0:
                base_cell, fraction = cell_idx - 1, 2.0 / 3.0
            elif phase_idx == 1:
                base_cell, fraction = cell_idx, 0.0
            else:
                base_cell, fraction = cell_idx, 1.0 / 3.0
            coeffs = ((-fraction ** 3 + 2 * fraction ** 2 - fraction) / 2,
                      (3 * fraction ** 3 - 5 * fraction ** 2 + 2) / 2,
                      (-3 * fraction ** 3 + 4 * fraction ** 2 + fraction) / 2,
                      (fraction ** 3 - fraction ** 2) / 2)
            for offset in range(4):
                weights[base_cell + 1 + offset, 3 * cell_idx + phase_idx] += coeffs[offset]
    return np.kron(weights, weights).astype(np.float32)


def coriolis_rows(row_index, total_rows):
    degrees = BASE_LATITUDE + (row_index.astype(jnp.float32) + 0.5) * ROW_DEGREES
    latitude = degrees * (math.pi / 180.0)
    return (ROTATION * jnp.sin(latitude))[:, None]


def step_fields(fields, east_cell, west_cell, north_cell, south_cell, coriolis, sea_mask):
    zonal_vel = fields[0]
    merid_vel = fields[1]
    grad_x = 0.5 * (east_cell - west_cell)
    grad_y = 0.5 * (north_cell - south_cell)
    laplace = east_cell + west_cell + north_cell + south_cell - 4.0 * fields
    advect = zonal_vel[None] * grad_x + merid_vel[None] * grad_y
    zonal_out = sea_mask * (zonal_vel - ADVECT * advect[0] + coriolis * merid_vel - PRESSURE * grad_x[2] + DIFFUSE * laplace[0])
    merid_out = sea_mask * (merid_vel - ADVECT * advect[1] - coriolis * zonal_vel - PRESSURE * grad_y[2] + DIFFUSE * laplace[1])
    tracer_out = sea_mask * (fields[2] - ADVECT * advect[2] + DIFFUSE * laplace[2])
    return zonal_out, merid_out, tracer_out


def cut_axis(source, blocks):
    lead = source.shape[:-1]
    head_part = source[..., :TILE * blocks].reshape(lead + (blocks, TILE))
    tail_part = source[..., 4:TILE * blocks + 4].reshape(lead + (blocks, TILE))[..., TILE - 4:]
    return jnp.concatenate([head_part, tail_part], axis=-1)


def cut_rims(widened, blocks_y, blocks_x):
    by_column = cut_axis(widened, blocks_x)
    by_column = jnp.moveaxis(by_column, 1, -1)
    both_cut = cut_axis(by_column, blocks_y)
    both_cut = jnp.transpose(both_cut, (3, 1, 0, 4, 2))
    return both_cut.reshape(blocks_y * blocks_x, widened.shape[0], (TILE + 4) * (TILE + 4))


def remap_levels(pieces, edge_list):
    lower_edge = edge_list[:, :-1]
    upper_edge = edge_list[:, 1:]
    level_idx = jnp.arange(pieces.shape[1], dtype=jnp.int32)
    inside = (level_idx[None, None, :] >= lower_edge[..., None]) & (level_idx[None, None, :] < upper_edge[..., None])
    weights = inside.astype(jnp.float32) / (upper_edge - lower_edge).astype(jnp.float32)[..., None]
    return jnp.einsum("nsk,nkc->nsc", weights, pieces, precision=lax.Precision.HIGHEST)


def reference(zonal_velocity, meridional_velocity, tracer, land_mask, remap_bounds, nest_owner):
    fields = jnp.stack([zonal_velocity, meridional_velocity, tracer])
    east_cell = jnp.roll(fields, -1, axis=-1)
    west_cell = jnp.roll(fields, 1, axis=-1)
    zero_row = jnp.zeros_like(fields[..., :1, :])
    north_cell = jnp.concatenate([fields[..., 1:, :], zero_row], axis=-2)
    south_cell = jnp.concatenate([zero_row, fields[..., :-1, :]], axis=-2)
    coriolis = coriolis_rows(jnp.arange(NY, dtype=jnp.int32), NY)
    sea_mask = land_mask.astype(jnp.float32)
    zonal_out, merid_out, tracer_out = step_fields(fields, east_cell, west_cell, north_cell, south_cell, coriolis, sea_mask)

    widened = jnp.concatenate([tracer_out[..., -2:], tracer_out, tracer_out[..., :2]], axis=-1)
    widened = jnp.pad(widened, ((0, 0), (2, 2), (0, 0)))
    interp = jnp.asarray(cubic_weights(TILE), jnp.float32)
    per_dev = BLK_Y * BLK_X

    def one_band(band_index):
        band_rows = lax.dynamic_slice_in_dim(widened, band_index * CELLS_Y, CELLS_Y + 4, 1)
        rim_blocks = cut_rims(band_rows, BLK_Y, NBX)
        rim_blocks = rim_blocks.reshape(BLK_Y, N_LON, BLK_X, LEVELS, RIM).transpose(1, 0, 2, 3, 4).reshape(N_LON * per_dev, LEVELS, RIM)
        band_bounds = lax.dynamic_slice_in_dim(remap_bounds, band_index * BLK_Y, BLK_Y, 0)
        band_bounds = band_bounds.reshape(BLK_Y, N_LON, BLK_X, SIGMA + 1).transpose(1, 0, 2, 3).reshape(N_LON * per_dev, SIGMA + 1)
        band_owner = lax.dynamic_slice_in_dim(nest_owner, band_index * BLK_Y, BLK_Y, 0)
        owners_dev = band_owner.reshape(BLK_Y, N_LON, BLK_X).transpose(1, 0, 2).reshape(N_LON, per_dev)
        sigma_blocks = remap_levels(rim_blocks, band_bounds)
        nest_values = jnp.einsum("nsc,cj->nsj", sigma_blocks, interp, precision=lax.Precision.HIGHEST)
        onehot = (owners_dev[..., None] == jnp.arange(N_LON + 1, dtype=jnp.int32)).astype(jnp.int32)
        before = jnp.cumsum(onehot, axis=1) - onehot
        rank_of = jnp.sum(before * onehot, axis=-1)
        source_lon = jnp.arange(N_LON, dtype=jnp.int32)[:, None]
        target = jnp.where(owners_dev < N_LON, owners_dev * SLOTS + source_lon * CAP + rank_of, N_LON * SLOTS).astype(jnp.int32)
        result = jnp.zeros((N_LON * SLOTS + 1, SIGMA, NCELL), jnp.float32).at[target.reshape(-1)].set(nest_values)
        return result[:-1].reshape(N_LON, SLOTS, SIGMA, NCELL)

    nest_tiles = lax.map(one_band, jnp.arange(N_LAT, dtype=jnp.int32))
    return zonal_out, merid_out, tracer_out, nest_tiles
```

```python
import functools
import math

import jax
import jax.numpy as jnp
import numpy as np
from jax import lax
from jax.experimental import pallas as pl
from jax.experimental.pallas import tpu as pltpu
from jax.sharding import PartitionSpec as P

SIGMA = 30
SIGMA_PAD = 32
TILE = 12
CAP = 2
BLK_X = 32
BLK_Y = 2
RIM = 256
NCELL = 1296
LEVEL_PAD = 80
CHUNK = 15

ADVECT = 0.25
DIFFUSE = 0.15
PRESSURE = 0.3
ROTATION = 0.6
BASE_LATITUDE = 20.0
ROW_DEGREES = 1.0 / 12.0

PARAMS = pltpu.CompilerParams(vmem_limit_bytes=48 * 2**20)


def cubic_weights(tile_cells):
    span_len = tile_cells + 4
    weights = np.zeros((span_len, 3 * tile_cells), np.float32)
    for cell_idx in range(tile_cells):
        for phase_idx in range(3):
            if phase_idx == 0:
                base_cell, fraction = (cell_idx - 1, 2.0 / 3.0)
            elif phase_idx == 1:
                base_cell, fraction = (cell_idx, 0.0)
            else:
                base_cell, fraction = (cell_idx, 1.0 / 3.0)
            coeffs = (
                (-(fraction**3) + 2 * fraction**2 - fraction) / 2,
                (3 * fraction**3 - 5 * fraction**2 + 2) / 2,
                (-3 * fraction**3 + 4 * fraction**2 + fraction) / 2,
                (fraction**3 - fraction**2) / 2,
            )
            for offset in range(4):
                weights[base_cell + 1 + offset, 3 * cell_idx + phase_idx] += coeffs[offset]
    return np.kron(weights, weights).astype(np.float32)


def coriolis_rows(row_index):
    degrees = BASE_LATITUDE + (row_index.astype(jnp.float32) + 0.5) * ROW_DEGREES
    latitude = degrees * (math.pi / 180.0)
    return (ROTATION * jnp.sin(latitude))[:, None]


def whole(shape):
    return pl.BlockSpec(shape, lambda i: (0,) * len(shape))


def pack_kernel(u_ref, v_ref, t_ref, first_row, last_row, first_col, last_col):
    step = pl.program_id(0)
    rows, cols = u_ref.shape[1:]
    lane = lax.broadcasted_iota(jnp.int32, (rows, 128), 1)

    @pl.when(step == 0)
    def _():
        first_row[...] = jnp.zeros_like(first_row)
        last_row[...] = jnp.zeros_like(last_row)
        first_col[...] = jnp.zeros_like(first_col)
        last_col[...] = jnp.zeros_like(last_col)

    for f, ref in enumerate((u_ref, v_ref, t_ref)):
        west = first_col[f]
        east = last_col[f]
        for i in range(CHUNK):
            k = step * CHUNK + i
            first_row[pl.ds(f * LEVEL_PAD + k, 1), :] = ref[i, 0:1, :]
            last_row[pl.ds(f * LEVEL_PAD + k, 1), :] = ref[i, rows - 1 : rows, :]
            here = lane == k
            west = jnp.where(here, ref[i, :, 0:128][:, 0:1], west)
            east = jnp.where(here, ref[i, :, cols - 128 : cols][:, 127:128], east)
        first_col[f] = west
        last_col[f] = east


def neighbours(x, f, k, east_ref, west_ref, north_ref, south_ref):
    rows, cols = x.shape
    col = lax.broadcasted_iota(jnp.int32, (rows, cols), 1)
    row = lax.broadcasted_iota(jnp.int32, (rows, cols), 0)
    e_col = pltpu.roll(east_ref[f], 127 - k, axis=1)[:, 127:128]
    w_col = pltpu.roll(west_ref[f], 127 - k, axis=1)[:, 127:128]
    n_row = north_ref[pl.ds(f * LEVEL_PAD + k, 1), :]
    s_row = south_ref[pl.ds(f * LEVEL_PAD + k, 1), :]
    east = jnp.where(col == cols - 1, e_col, pltpu.roll(x, cols - 1, axis=1))
    west = jnp.where(col == 0, w_col, pltpu.roll(x, 1, axis=1))
    north = jnp.where(row == rows - 1, n_row, pltpu.roll(x, rows - 1, axis=0))
    south = jnp.where(row == 0, s_row, pltpu.roll(x, 1, axis=0))
    return 0.5 * (east - west), 0.5 * (north - south), east + west + north + south - 4.0 * x


def tracer_kernel(
    u_ref, v_ref, t_ref, mask_ref, east_ref, west_ref, north_ref, south_ref,
    out_ref, tiles, low_rows, high_rows, west_cols, east_cols,
):
    step = pl.program_id(0)
    rows, cols = u_ref.shape[1:]
    sea = mask_ref[...].astype(jnp.float32)
    for i in range(CHUNK):
        k = step * CHUNK + i
        t = t_ref[i]
        gx, gy, lap = neighbours(t, 2, k, east_ref, west_ref, north_ref, south_ref)
        advect = u_ref[i] * gx + v_ref[i] * gy
        new = sea * (t - ADVECT * advect + DIFFUSE * lap)
        out_ref[i] = new
        for c in range(cols // 128):
            tiles[c, pl.ds(pl.multiple_of(k * rows, 8), rows), :] = new[:, c * 128 : c * 128 + 128]

    @pl.when(step == pl.num_programs(0) - 1)
    def _():
        count = tiles.shape[1] // rows
        lane = lax.broadcasted_iota(jnp.int32, (count, 128), 1)
        low_rows[...] = jnp.zeros_like(low_rows)
        high_rows[...] = jnp.zeros_like(high_rows)
        west_cols[...] = jnp.zeros_like(west_cols)
        east_cols[...] = jnp.zeros_like(east_cols)
        for r in range(2):
            for c in range(0, cols, 128):
                low_rows[r * LEVEL_PAD : r * LEVEL_PAD + count, c : c + 128] = tiles[
                    c // 128, pl.ds(r, count, stride=rows), :
                ]
                high_rows[r * LEVEL_PAD : r * LEVEL_PAD + count, c : c + 128] = tiles[
                    c // 128, pl.ds(rows - 2 + r, count, stride=rows), :
                ]
        west = jnp.zeros((count, 128), jnp.float32)
        east = jnp.zeros((count, 128), jnp.float32)
        for r in range(rows):
            here = (lane >= 2 * r) & (lane < 2 * r + 2)
            w = tiles[0, pl.ds(r, count, stride=rows), :]
            e = tiles[cols // 128 - 1, pl.ds(r, count, stride=rows), :]
            west = jnp.where(here, pltpu.roll(w, 2 * r, axis=1) if r else w, west)
            east = jnp.where(here, pltpu.roll(e, 2 * r + 2, axis=1), east)
        west_cols[0:count, :] = west
        east_cols[0:count, :] = east


def momentum_kernel(
    u_ref, v_ref, t_ref, mask_ref, coriolis_ref, east_ref, west_ref, north_ref, south_ref,
    zonal_ref, merid_ref,
):
    step = pl.program_id(0)
    sea = mask_ref[...].astype(jnp.float32)
    coriolis = coriolis_ref[...]
    halos = (east_ref, west_ref, north_ref, south_ref)
    for i in range(CHUNK):
        k = step * CHUNK + i
        u, v = u_ref[i], v_ref[i]
        t_gx, t_gy, _ = neighbours(t_ref[i], 2, k, *halos)
        gx, gy, lap = neighbours(u, 0, k, *halos)
        zonal_ref[i] = sea * (
            u - ADVECT * (u * gx + v * gy) + coriolis * v - PRESSURE * t_gx + DIFFUSE * lap
        )
        gx, gy, lap = neighbours(v, 1, k, *halos)
        merid_ref[i] = sea * (
            v - ADVECT * (u * gx + v * gy) - coriolis * u - PRESSURE * t_gy + DIFFUSE * lap
        )


def rim_kernel(
    block_ref, x_ref, east_ref, west_ref, north_ref, south_ref, corner_n, corner_s, inside_ref,
    out_ref, wide, rim,
):
    levels = inside_ref.shape[2]
    cols = x_ref.shape[0] * 128
    rows = x_ref.shape[1] // levels
    lane = lax.broadcasted_iota(jnp.int32, (levels, 128), 1)

    def side(east, west, r):
        e = pltpu.roll(east, 128 - 2 * r, axis=1) if r else east
        w = pltpu.roll(west, 126 - 2 * r, axis=1)
        return jnp.where(lane < 64, e, w)

    for r in range(rows):
        for c in range(0, cols, 128):
            wide[r + 2, 0:levels, c : c + 128] = x_ref[c // 128, pl.ds(r, levels, stride=rows), :]
        wide[r + 2, 0:levels, cols : cols + 128] = side(
            east_ref[0:levels, :], west_ref[0:levels, :], r
        )
    for j in range(2):
        at = slice(j * LEVEL_PAD, j * LEVEL_PAD + levels)
        wide[j, 0:levels, 0:cols] = south_ref[at, :]
        wide[j, 0:levels, cols : cols + 128] = side(
            corner_s[0, 0:levels, :], corner_s[1, 0:levels, :], rows - 2 + j
        )
        wide[rows + 2 + j, 0:levels, 0:cols] = north_ref[at, :]
        wide[rows + 2 + j, 0:levels, cols : cols + 128] = side(
            corner_n[0, 0:levels, :], corner_n[1, 0:levels, :], j
        )

    ring = cols + 128

    def slot(s, carry):
        b = block_ref[s]
        by, bx = b // BLK_X, b % BLK_X
        start = (TILE * bx - 2 + ring) % ring
        first, off = start // 128, start % 128
        second = (first + 1) % (ring // 128)
        first = pl.multiple_of(first * 128, 128)
        second = pl.multiple_of(second * 128, 128)
        for half in range(2):
            acc = jnp.zeros((levels, 128), jnp.float32)
            for q in range(8):
                r = by * TILE + half * 8 + q
                a = wide[r, 0:levels, pl.ds(first, 128)]
                z = wide[r, 0:levels, pl.ds(second, 128)]
                both = jnp.where(lane >= off, a, z)
                both = pltpu.roll(both, (16 * q - off + 128) % 128, axis=1)
                acc = jnp.where((lane >= 16 * q) & (lane < 16 * q + 16), both, acc)
            rim[0:levels, half * 128 : half * 128 + 128] = acc
        inside = inside_ref[s]
        x = rim[0:levels, :]
        high = x.astype(jnp.bfloat16)
        low = (x - high.astype(jnp.float32)).astype(jnp.bfloat16)
        ones = inside.astype(jnp.bfloat16)
        total = jnp.dot(ones, high, preferred_element_type=jnp.float32) + jnp.dot(
            ones, low, preferred_element_type=jnp.float32
        )
        count = jnp.sum(inside, axis=1, keepdims=True)
        total = total / jnp.maximum(count, 1.0)
        out_ref[s, 0] = total[:, 0:128]
        out_ref[s, 1] = total[:, 128:256]
        return carry

    lax.fori_loop(0, out_ref.shape[0], slot, 0)


def interp_kernel(x_ref, high_ref, low_ref, out_ref):
    slots = x_ref.shape[0] // (2 * SIGMA_PAD)
    per_step = out_ref.shape[0] // slots
    step = pl.program_id(0)
    for i in range(per_step):
        s = step * per_step + i
        halves = [
            x_ref[pl.ds(h * SIGMA_PAD + s, slots, stride=2 * SIGMA_PAD), :] for h in range(2)
        ]
        x = jnp.concatenate(halves, axis=1)
        high = x.astype(jnp.bfloat16)
        low = (x - high.astype(jnp.float32)).astype(jnp.bfloat16)
        both = jnp.concatenate([high, low], axis=0)
        wide = jnp.dot(both, high_ref[...], preferred_element_type=jnp.float32)
        out_ref[i * slots : (i + 1) * slots, :] = (
            wide[:slots]
            + wide[slots:]
            + jnp.dot(high, low_ref[...], preferred_element_type=jnp.float32)
        )


def shift(x, axis, wrap, forward):
    count = lax.axis_size(axis)
    up = [(i, (i + 1) % count) for i in range(count if wrap else count - 1)]
    return lax.ppermute(x, axis, up if forward else [(j, i) for i, j in up])


def per_device(zonal_velocity, meridional_velocity, tracer, land_mask, remap_bounds, nest_owner):
    levels, rows, cols = tracer.shape
    lon_count = lax.axis_size("lon")
    slots = CAP * lon_count
    steps = levels // CHUNK
    f32 = jnp.float32
    fields = (zonal_velocity, meridional_velocity, tracer)
    field_spec = pl.BlockSpec((CHUNK, rows, cols), lambda i: (i, 0, 0))
    row_shape, col_shape = (3 * LEVEL_PAD, cols), (3, rows, 128)
    field_bytes = levels * rows * cols * 4

    first_row, last_row, first_col, last_col = pl.pallas_call(
        pack_kernel,
        grid=(steps,),
        in_specs=[field_spec] * 3,
        out_specs=[whole(row_shape)] * 2 + [whole(col_shape)] * 2,
        out_shape=[jax.ShapeDtypeStruct(row_shape, f32)] * 2
        + [jax.ShapeDtypeStruct(col_shape, f32)] * 2,
        compiler_params=PARAMS,
        name="pack_edges",
    )(*fields)
    north = shift(first_row, "lat", False, False)
    south = shift(last_row, "lat", False, True)
    east = shift(first_col, "lon", True, False)
    west = shift(last_col, "lon", True, True)
    halos = (east, west, north, south)
    halo_specs = [whole(col_shape)] * 2 + [whole(row_shape)] * 2

    margin_row, margin_col = (2 * LEVEL_PAD, cols), (LEVEL_PAD, 128)
    tile_shape = (cols // 128, levels * rows, 128)
    tracer_new, tiles, low_rows, high_rows, west_cols, east_cols = pl.pallas_call(
        tracer_kernel,
        grid=(steps,),
        in_specs=[field_spec] * 3 + [whole((rows, cols))] + halo_specs,
        out_specs=[field_spec, whole(tile_shape)] + [whole(margin_row)] * 2 + [whole(margin_col)] * 2,
        out_shape=[jax.ShapeDtypeStruct(s, f32) for s in (tracer.shape, tile_shape)]
        + [jax.ShapeDtypeStruct(margin_row, f32)] * 2
        + [jax.ShapeDtypeStruct(margin_col, f32)] * 2,
        compiler_params=PARAMS,
        name="tracer_step",
    )(*fields, land_mask, *halos)
    east_margin = shift(west_cols, "lon", True, False)
    west_margin = shift(east_cols, "lon", True, True)
    north_margin = shift(low_rows, "lat", False, False)
    south_margin = shift(high_rows, "lat", False, True)
    sides = jnp.stack([east_margin, west_margin])
    corner_n = shift(sides, "lat", False, False)
    corner_s = shift(sides, "lat", False, True)

    row_index = lax.axis_index("lat") * rows + jnp.arange(rows, dtype=jnp.int32)
    coriolis = jnp.broadcast_to(coriolis_rows(row_index), (rows, cols))
    zonal_new, merid_new = pl.pallas_call(
        momentum_kernel,
        grid=(steps,),
        in_specs=[field_spec] * 3 + [whole((rows, cols))] * 2 + halo_specs,
        out_specs=[field_spec] * 2,
        out_shape=[jax.ShapeDtypeStruct(tracer.shape, f32)] * 2,
        compiler_params=PARAMS,
        cost_estimate=pl.CostEstimate(
            flops=60 * levels * rows * cols, bytes_accessed=5 * field_bytes, transcendentals=0
        ),
        name="momentum_step",
    )(*fields, land_mask, coriolis, *halos)

    per_dev = BLK_Y * BLK_X
    owners = nest_owner.reshape(per_dev)
    bounds = remap_bounds.reshape(per_dev, SIGMA + 1)
    number = jnp.arange(per_dev, dtype=jnp.int32)
    earlier = (owners[None, :] == owners[:, None]) & (number[None, :] < number[:, None])
    rank_of = jnp.sum(earlier.astype(jnp.int32), axis=1)
    target = jnp.where(owners < lon_count, owners * CAP + rank_of, slots)
    chosen = (target[None, :] == jnp.arange(slots, dtype=jnp.int32)[:, None]).astype(jnp.int32)
    block_of = jnp.sum(chosen * number[None, :], axis=1)
    edges = jnp.sum(chosen[:, :, None] * bounds[None], axis=1)
    edges = jnp.pad(edges, ((0, 0), (0, SIGMA_PAD - SIGMA)), mode="edge")
    level = jnp.arange(levels, dtype=jnp.int32)[None, None, :]
    inside = ((level >= edges[:, :-1, None]) & (level < edges[:, 1:, None])).astype(f32)

    vmem = pl.BlockSpec(memory_space=pltpu.VMEM)
    sigma_blocks = pl.pallas_call(
        rim_kernel,
        in_specs=[pl.BlockSpec(memory_space=pltpu.SMEM)] + [vmem] * 8,
        out_specs=vmem,
        out_shape=jax.ShapeDtypeStruct((slots, 2, SIGMA_PAD, 128), f32),
        scratch_shapes=[
            pltpu.VMEM((rows + 4, LEVEL_PAD, cols + 128), f32),
            pltpu.VMEM((LEVEL_PAD, RIM), f32),
        ],
        compiler_params=PARAMS,
        name="sigma_rims",
    )(
        block_of, tiles, east_margin, west_margin, north_margin, south_margin,
        corner_n, corner_s,
        jnp.pad(inside, ((0, 0), (0, SIGMA_PAD - inside.shape[1]), (0, 0))),
    )
    received = lax.all_to_all(
        sigma_blocks.reshape(lon_count, CAP * 2 * SIGMA_PAD, 128),
        "lon", split_axis=0, concat_axis=0, tiled=True,
    )

    table = cubic_weights(TILE)
    high = jnp.asarray(table).astype(jnp.bfloat16)
    low = (jnp.asarray(table) - high.astype(f32)).astype(jnp.bfloat16)
    per_step = 6
    nest = pl.pallas_call(
        interp_kernel,
        grid=(SIGMA // per_step,),
        in_specs=[whole((slots * 2 * SIGMA_PAD, 128))] + [whole((RIM, NCELL))] * 2,
        out_specs=pl.BlockSpec((per_step * slots, NCELL), lambda i: (i, 0)),
        out_shape=jax.ShapeDtypeStruct((SIGMA * slots, NCELL), f32),
        compiler_params=PARAMS,
        name="interpolate",
    )(received.reshape(slots * 2 * SIGMA_PAD, 128), high, low)
    nest = nest.reshape(SIGMA, slots, NCELL).transpose(1, 0, 2)
    return (
        zonal_new,
        merid_new,
        tracer_new,
        nest.reshape(1, 1, slots, SIGMA, NCELL),
    )


def solution(mesh):
    return jax.shard_map(
        per_device,
        mesh=mesh,
        in_specs=(
            P(None, "lat", "lon"),
            P(None, "lat", "lon"),
            P(None, "lat", "lon"),
            P("lat", "lon"),
            P("lat", "lon", None),
            P("lat", "lon"),
        ),
        out_specs=(
            P(None, "lat", "lon"),
            P(None, "lat", "lon"),
            P(None, "lat", "lon"),
            P("lat", "lon", None, None, None),
        ),
        check_vma=False,
    )
```

```python
import functools
import math

import jax
import jax.numpy as jnp
import numpy as np
from jax import lax
from jax.experimental import pallas as pl
from jax.experimental.pallas import tpu as pltpu
from jax.sharding import PartitionSpec as P

SIGMA = 30
SIGMA_PAD = 32
TILE = 12
CAP = 2
BLK_X = 32
BLK_Y = 2
RIM = 256
NCELL = 1296
LEVEL_PAD = 80
CHUNK = 15

ADVECT = 0.25
DIFFUSE = 0.15
PRESSURE = 0.3
ROTATION = 0.6
BASE_LATITUDE = 20.0
ROW_DEGREES = 1.0 / 12.0

PARAMS = pltpu.CompilerParams(vmem_limit_bytes=48 * 2**20)


def cubic_weights(tile_cells):
    span_len = tile_cells + 4
    weights = np.zeros((span_len, 3 * tile_cells), np.float32)
    for cell_idx in range(tile_cells):
        for phase_idx in range(3):
            if phase_idx == 0:
                base_cell, fraction = (cell_idx - 1, 2.0 / 3.0)
            elif phase_idx == 1:
                base_cell, fraction = (cell_idx, 0.0)
            else:
                base_cell, fraction = (cell_idx, 1.0 / 3.0)
            coeffs = (
                (-(fraction**3) + 2 * fraction**2 - fraction) / 2,
                (3 * fraction**3 - 5 * fraction**2 + 2) / 2,
                (-3 * fraction**3 + 4 * fraction**2 + fraction) / 2,
                (fraction**3 - fraction**2) / 2,
            )
            for offset in range(4):
                weights[base_cell + 1 + offset, 3 * cell_idx + phase_idx] += coeffs[offset]
    return np.kron(weights, weights).astype(np.float32)


def coriolis_rows(row_index):
    degrees = BASE_LATITUDE + (row_index.astype(jnp.float32) + 0.5) * ROW_DEGREES
    latitude = degrees * (math.pi / 180.0)
    return (ROTATION * jnp.sin(latitude))[:, None]


def whole(shape):
    return pl.BlockSpec(shape, lambda i: (0,) * len(shape))


def pack_kernel(u_ref, v_ref, t_ref, first_row, last_row, first_col, last_col):
    step = pl.program_id(0)
    rows, cols = u_ref.shape[1:]
    lane = lax.broadcasted_iota(jnp.int32, (rows, 128), 1)

    @pl.when(step == 0)
    def _():
        first_row[...] = jnp.zeros_like(first_row)
        last_row[...] = jnp.zeros_like(last_row)
        first_col[...] = jnp.zeros_like(first_col)
        last_col[...] = jnp.zeros_like(last_col)

    for f, ref in enumerate((u_ref, v_ref, t_ref)):
        west = first_col[f]
        east = last_col[f]
        for i in range(CHUNK):
            k = step * CHUNK + i
            first_row[pl.ds(f * LEVEL_PAD + k, 1), :] = ref[i, 0:1, :]
            last_row[pl.ds(f * LEVEL_PAD + k, 1), :] = ref[i, rows - 1 : rows, :]
            here = lane == k
            west = jnp.where(here, ref[i, :, 0:128][:, 0:1], west)
            east = jnp.where(here, ref[i, :, cols - 128 : cols][:, 127:128], east)
        first_col[f] = west
        last_col[f] = east


def neighbours(x, f, k, east_ref, west_ref, north_ref, south_ref):
    rows, cols = x.shape
    lane = lax.broadcasted_iota(jnp.int32, (rows, 128), 1)
    row = lax.broadcasted_iota(jnp.int32, (8, cols), 0)
    e_col = pltpu.roll(east_ref[f], 127 - k, axis=1)[:, 127:128]
    w_col = pltpu.roll(west_ref[f], 127 - k, axis=1)[:, 127:128]
    n_row = north_ref[pl.ds(f * LEVEL_PAD + k, 1), :]
    s_row = south_ref[pl.ds(f * LEVEL_PAD + k, 1), :]
    east = pltpu.roll(x, cols - 1, axis=1)
    tail = jnp.where(lane == 127, e_col, east[:, cols - 128 :])
    east = jnp.concatenate([east[:, : cols - 128], tail], axis=1)
    west = pltpu.roll(x, 1, axis=1)
    head = jnp.where(lane == 0, w_col, west[:, :128])
    west = jnp.concatenate([head, west[:, 128:]], axis=1)
    north = pltpu.roll(x, rows - 1, axis=0)
    tail = jnp.where(row == 7, n_row, north[rows - 8 :])
    north = jnp.concatenate([north[: rows - 8], tail], axis=0)
    south = pltpu.roll(x, 1, axis=0)
    head = jnp.where(row == 0, s_row, south[:8])
    south = jnp.concatenate([head, south[8:]], axis=0)
    return 0.5 * (east - west), 0.5 * (north - south), east + west + north + south - 4.0 * x


def tracer_kernel(
    u_ref, v_ref, t_ref, mask_ref, east_ref, west_ref, north_ref, south_ref,
    out_ref, tiles, low_rows, high_rows, west_cols, east_cols,
):
    step = pl.program_id(0)
    rows, cols = u_ref.shape[1:]
    sea = mask_ref[...].astype(jnp.float32)
    for i in range(CHUNK):
        k = step * CHUNK + i
        t = t_ref[i]
        gx, gy, lap = neighbours(t, 2, k, east_ref, west_ref, north_ref, south_ref)
        advect = u_ref[i] * gx + v_ref[i] * gy
        new = sea * (t - ADVECT * advect + DIFFUSE * lap)
        out_ref[i] = new
        for c in range(cols // 128):
            tiles[c, pl.ds(pl.multiple_of(k * rows, 8), rows), :] = new[:, c * 128 : c * 128 + 128]

    @pl.when(step == pl.num_programs(0) - 1)
    def _():
        count = tiles.shape[1] // rows
        lane = lax.broadcasted_iota(jnp.int32, (count, 128), 1)
        low_rows[...] = jnp.zeros_like(low_rows)
        high_rows[...] = jnp.zeros_like(high_rows)
        west_cols[...] = jnp.zeros_like(west_cols)
        east_cols[...] = jnp.zeros_like(east_cols)
        for r in range(2):
            for c in range(0, cols, 128):
                low_rows[r * LEVEL_PAD : r * LEVEL_PAD + count, c : c + 128] = tiles[
                    c // 128, pl.ds(r, count, stride=rows), :
                ]
                high_rows[r * LEVEL_PAD : r * LEVEL_PAD + count, c : c + 128] = tiles[
                    c // 128, pl.ds(rows - 2 + r, count, stride=rows), :
                ]
        west = jnp.zeros((count, 128), jnp.float32)
        east = jnp.zeros((count, 128), jnp.float32)
        for r in range(rows):
            here = (lane >= 2 * r) & (lane < 2 * r + 2)
            w = tiles[0, pl.ds(r, count, stride=rows), :]
            e = tiles[cols // 128 - 1, pl.ds(r, count, stride=rows), :]
            west = jnp.where(here, pltpu.roll(w, 2 * r, axis=1) if r else w, west)
            east = jnp.where(here, pltpu.roll(e, 2 * r + 2, axis=1), east)
        west_cols[0:count, :] = west
        east_cols[0:count, :] = east


def momentum_kernel(
    u_ref, v_ref, t_ref, mask_ref, coriolis_ref, east_ref, west_ref, north_ref, south_ref,
    zonal_ref, merid_ref,
):
    step = pl.program_id(0)
    sea = mask_ref[...].astype(jnp.float32)
    coriolis = coriolis_ref[...]
    halos = (east_ref, west_ref, north_ref, south_ref)
    for i in range(CHUNK):
        k = step * CHUNK + i
        u, v = u_ref[i], v_ref[i]
        t_gx, t_gy, _ = neighbours(t_ref[i], 2, k, *halos)
        gx, gy, lap = neighbours(u, 0, k, *halos)
        zonal_ref[i] = sea * (
            u - ADVECT * (u * gx + v * gy) + coriolis * v - PRESSURE * t_gx + DIFFUSE * lap
        )
        gx, gy, lap = neighbours(v, 1, k, *halos)
        merid_ref[i] = sea * (
            v - ADVECT * (u * gx + v * gy) - coriolis * u - PRESSURE * t_gy + DIFFUSE * lap
        )


def rim_kernel(
    block_ref, x_ref, east_ref, west_ref, north_ref, south_ref, corner_n, corner_s, inside_ref,
    out_ref, wide, rim,
):
    levels = inside_ref.shape[2]
    cols = x_ref.shape[0] * 128
    rows = x_ref.shape[1] // levels
    lane = lax.broadcasted_iota(jnp.int32, (levels, 128), 1)

    def side(east, west, r):
        e = pltpu.roll(east, 128 - 2 * r, axis=1) if r else east
        w = pltpu.roll(west, 126 - 2 * r, axis=1)
        return jnp.where(lane < 64, e, w)

    for r in range(rows):
        for c in range(0, cols, 128):
            wide[r + 2, 0:levels, c : c + 128] = x_ref[c // 128, pl.ds(r, levels, stride=rows), :]
        wide[r + 2, 0:levels, cols : cols + 128] = side(
            east_ref[0:levels, :], west_ref[0:levels, :], r
        )
    for j in range(2):
        at = slice(j * LEVEL_PAD, j * LEVEL_PAD + levels)
        wide[j, 0:levels, 0:cols] = south_ref[at, :]
        wide[j, 0:levels, cols : cols + 128] = side(
            corner_s[0, 0:levels, :], corner_s[1, 0:levels, :], rows - 2 + j
        )
        wide[rows + 2 + j, 0:levels, 0:cols] = north_ref[at, :]
        wide[rows + 2 + j, 0:levels, cols : cols + 128] = side(
            corner_n[0, 0:levels, :], corner_n[1, 0:levels, :], j
        )

    ring = cols + 128

    def slot(s, carry):
        b = block_ref[s]
        by, bx = b // BLK_X, b % BLK_X
        start = (TILE * bx - 2 + ring) % ring
        first, off = start // 128, start % 128
        second = (first + 1) % (ring // 128)
        first = pl.multiple_of(first * 128, 128)
        second = pl.multiple_of(second * 128, 128)
        for half in range(2):
            acc = jnp.zeros((levels, 128), jnp.float32)
            for q in range(8):
                r = by * TILE + half * 8 + q
                a = wide[r, 0:levels, pl.ds(first, 128)]
                z = wide[r, 0:levels, pl.ds(second, 128)]
                both = jnp.where(lane >= off, a, z)
                both = pltpu.roll(both, (16 * q - off + 128) % 128, axis=1)
                acc = jnp.where((lane >= 16 * q) & (lane < 16 * q + 16), both, acc)
            rim[0:levels, half * 128 : half * 128 + 128] = acc
        inside = inside_ref[s]
        x = rim[0:levels, :]
        high = x.astype(jnp.bfloat16)
        low = (x - high.astype(jnp.float32)).astype(jnp.bfloat16)
        ones = inside.astype(jnp.bfloat16)
        total = jnp.dot(ones, high, preferred_element_type=jnp.float32) + jnp.dot(
            ones, low, preferred_element_type=jnp.float32
        )
        count = jnp.sum(inside, axis=1, keepdims=True)
        total = total / jnp.maximum(count, 1.0)
        out_ref[s, 0] = total[:, 0:128]
        out_ref[s, 1] = total[:, 128:256]
        return carry

    lax.fori_loop(0, out_ref.shape[0], slot, 0)


def interp_kernel(x_ref, high_ref, low_ref, out_ref):
    slots = x_ref.shape[0] // (2 * SIGMA_PAD)
    per_step = out_ref.shape[0] // slots
    step = pl.program_id(0)
    for i in range(per_step):
        s = step * per_step + i
        halves = [
            x_ref[pl.ds(h * SIGMA_PAD + s, slots, stride=2 * SIGMA_PAD), :] for h in range(2)
        ]
        x = jnp.concatenate(halves, axis=1)
        high = x.astype(jnp.bfloat16)
        low = (x - high.astype(jnp.float32)).astype(jnp.bfloat16)
        both = jnp.concatenate([high, low], axis=0)
        wide = jnp.dot(both, high_ref[...], preferred_element_type=jnp.float32)
        out_ref[i * slots : (i + 1) * slots, :] = (
            wide[:slots]
            + wide[slots:]
            + jnp.dot(high, low_ref[...], preferred_element_type=jnp.float32)
        )


def exchange_kernel(
    corners, first_row, last_row, first_col, last_col, north, south, east, west, *rest
):
    corner_n, corner_s = rest[:2] if corners else (None, None)
    send, recv = rest[-2:]
    lon_count, lat_count = lax.axis_size("lon"), lax.axis_size("lat")
    lon, lat = lax.axis_index("lon"), lax.axis_index("lat")
    right = (lax.rem(lon + 1, lon_count), lat)
    left = (lax.rem(lon + lon_count - 1, lon_count), lat)
    up = (lon, lax.rem(lat + 1, lat_count))
    down = (lon, lax.rem(lat + lat_count - 1, lat_count))
    mesh_id = pl.DeviceIdType.MESH
    has_up, has_down = lat < lat_count - 1, lat > 0
    barrier = pltpu.get_barrier_semaphore()

    def greet(device):
        pl.semaphore_signal(barrier, inc=1, device_id=device, device_id_type=mesh_id)

    greet(left)
    greet(right)
    pl.when(has_up)(lambda: greet(up))
    pl.when(has_down)(lambda: greet(down))
    pl.semaphore_wait(barrier, 2 + has_up.astype(jnp.int32) + has_down.astype(jnp.int32))

    def copy(n, src, dst, device):
        return pltpu.make_async_remote_copy(
            src_ref=src, dst_ref=dst, send_sem=send.at[n], recv_sem=recv.at[n],
            device_id=device, device_id_type=mesh_id,
        )

    to_west = copy(0, first_col, east, left)
    to_east = copy(1, last_col, west, right)
    to_down = [copy(2, first_row, north, down)]
    to_up = [copy(3, last_row, south, up)]
    to_west.start()
    to_east.start()
    pl.when(has_down)(lambda: to_down[0].start())
    pl.when(has_up)(lambda: to_up[0].start())
    to_west.wait()
    to_east.wait()
    if corners:
        for n, ref in enumerate((east, west)):
            to_down.append(copy(4 + n, ref, corner_n.at[n], down))
            to_up.append(copy(6 + n, ref, corner_s.at[n], up))

    @pl.when(has_down)
    def _():
        for c in to_down[1:]:
            c.start()

    @pl.when(has_up)
    def _():
        for c in to_up[1:]:
            c.start()

    @pl.when(has_down)
    def _():
        for c in to_down:
            c.wait_send()
        for c in to_up:
            c.wait_recv()

    @pl.when(has_up)
    def _():
        for c in to_up:
            c.wait_send()
        for c in to_down:
            c.wait_recv()

    @pl.when(jnp.logical_not(has_up))
    def _():
        north[...] = jnp.zeros_like(north)
        if corners:
            corner_n[...] = jnp.zeros_like(corner_n)

    @pl.when(jnp.logical_not(has_down))
    def _():
        south[...] = jnp.zeros_like(south)
        if corners:
            corner_s[...] = jnp.zeros_like(corner_s)


def exchange(first_row, last_row, first_col, last_col, corners):
    row, col = first_row.shape, first_col.shape
    shapes = [row, row, col, col] + ([(2,) + col] * 2 if corners else [])
    vmem = pl.BlockSpec(memory_space=pltpu.VMEM)
    sems = 8 if corners else 4
    return pl.pallas_call(
        functools.partial(exchange_kernel, corners),
        in_specs=[vmem] * 4,
        out_specs=[vmem] * len(shapes),
        out_shape=[jax.ShapeDtypeStruct(s, jnp.float32) for s in shapes],
        scratch_shapes=[pltpu.SemaphoreType.DMA((sems,)), pltpu.SemaphoreType.DMA((sems,))],
        compiler_params=pltpu.CompilerParams(
            collective_id=1 if corners else 0, has_side_effects=True
        ),
        name="exchange_margins" if corners else "exchange_edges",
    )(first_row, last_row, first_col, last_col)


def per_device(zonal_velocity, meridional_velocity, tracer, land_mask, remap_bounds, nest_owner):
    levels, rows, cols = tracer.shape
    lon_count = lax.axis_size("lon")
    slots = CAP * lon_count
    steps = levels // CHUNK
    f32 = jnp.float32
    fields = (zonal_velocity, meridional_velocity, tracer)
    field_spec = pl.BlockSpec((CHUNK, rows, cols), lambda i: (i, 0, 0))
    row_shape, col_shape = (3 * LEVEL_PAD, cols), (3, rows, 128)
    field_bytes = levels * rows * cols * 4

    first_row, last_row, first_col, last_col = pl.pallas_call(
        pack_kernel,
        grid=(steps,),
        in_specs=[field_spec] * 3,
        out_specs=[whole(row_shape)] * 2 + [whole(col_shape)] * 2,
        out_shape=[jax.ShapeDtypeStruct(row_shape, f32)] * 2
        + [jax.ShapeDtypeStruct(col_shape, f32)] * 2,
        compiler_params=PARAMS,
        name="pack_edges",
    )(*fields)
    north, south, east, west = exchange(first_row, last_row, first_col, last_col, False)
    halos = (east, west, north, south)
    halo_specs = [whole(col_shape)] * 2 + [whole(row_shape)] * 2

    margin_row, margin_col = (2 * LEVEL_PAD, cols), (LEVEL_PAD, 128)
    tile_shape = (cols // 128, levels * rows, 128)
    tracer_new, tiles, low_rows, high_rows, west_cols, east_cols = pl.pallas_call(
        tracer_kernel,
        grid=(steps,),
        in_specs=[field_spec] * 3 + [whole((rows, cols))] + halo_specs,
        out_specs=[field_spec, whole(tile_shape)] + [whole(margin_row)] * 2 + [whole(margin_col)] * 2,
        out_shape=[jax.ShapeDtypeStruct(s, f32) for s in (tracer.shape, tile_shape)]
        + [jax.ShapeDtypeStruct(margin_row, f32)] * 2
        + [jax.ShapeDtypeStruct(margin_col, f32)] * 2,
        compiler_params=PARAMS,
        name="tracer_step",
    )(*fields, land_mask, *halos)
    north_margin, south_margin, east_margin, west_margin, corner_n, corner_s = exchange(
        low_rows, high_rows, west_cols, east_cols, True
    )

    row_index = lax.axis_index("lat") * rows + jnp.arange(rows, dtype=jnp.int32)
    coriolis = jnp.broadcast_to(coriolis_rows(row_index), (rows, cols))
    zonal_new, merid_new = pl.pallas_call(
        momentum_kernel,
        grid=(steps,),
        in_specs=[field_spec] * 3 + [whole((rows, cols))] * 2 + halo_specs,
        out_specs=[field_spec] * 2,
        out_shape=[jax.ShapeDtypeStruct(tracer.shape, f32)] * 2,
        compiler_params=PARAMS,
        cost_estimate=pl.CostEstimate(
            flops=60 * levels * rows * cols, bytes_accessed=5 * field_bytes, transcendentals=0
        ),
        name="momentum_step",
    )(*fields, land_mask, coriolis, *halos)

    per_dev = BLK_Y * BLK_X
    owners = nest_owner.reshape(per_dev)
    bounds = remap_bounds.reshape(per_dev, SIGMA + 1)
    number = jnp.arange(per_dev, dtype=jnp.int32)
    earlier = (owners[None, :] == owners[:, None]) & (number[None, :] < number[:, None])
    rank_of = jnp.sum(earlier.astype(jnp.int32), axis=1)
    target = jnp.where(owners < lon_count, owners * CAP + rank_of, slots)
    chosen = (target[None, :] == jnp.arange(slots, dtype=jnp.int32)[:, None]).astype(jnp.int32)
    block_of = jnp.sum(chosen * number[None, :], axis=1)
    edges = jnp.sum(chosen[:, :, None] * bounds[None], axis=1)
    edges = jnp.pad(edges, ((0, 0), (0, SIGMA_PAD - SIGMA)), mode="edge")
    level = jnp.arange(levels, dtype=jnp.int32)[None, None, :]
    inside = ((level >= edges[:, :-1, None]) & (level < edges[:, 1:, None])).astype(f32)

    vmem = pl.BlockSpec(memory_space=pltpu.VMEM)
    sigma_blocks = pl.pallas_call(
        rim_kernel,
        in_specs=[pl.BlockSpec(memory_space=pltpu.SMEM)] + [vmem] * 8,
        out_specs=vmem,
        out_shape=jax.ShapeDtypeStruct((slots, 2, SIGMA_PAD, 128), f32),
        scratch_shapes=[
            pltpu.VMEM((rows + 4, LEVEL_PAD, cols + 128), f32),
            pltpu.VMEM((LEVEL_PAD, RIM), f32),
        ],
        compiler_params=PARAMS,
        name="sigma_rims",
    )(
        block_of, tiles, east_margin, west_margin, north_margin, south_margin,
        corner_n, corner_s,
        jnp.pad(inside, ((0, 0), (0, SIGMA_PAD - inside.shape[1]), (0, 0))),
    )
    received = lax.all_to_all(
        sigma_blocks.reshape(lon_count, CAP * 2 * SIGMA_PAD, 128),
        "lon", split_axis=0, concat_axis=0, tiled=True,
    )

    table = cubic_weights(TILE)
    high = jnp.asarray(table).astype(jnp.bfloat16)
    low = (jnp.asarray(table) - high.astype(f32)).astype(jnp.bfloat16)
    per_step = 6
    nest = pl.pallas_call(
        interp_kernel,
        grid=(SIGMA // per_step,),
        in_specs=[whole((slots * 2 * SIGMA_PAD, 128))] + [whole((RIM, NCELL))] * 2,
        out_specs=pl.BlockSpec((per_step * slots, NCELL), lambda i: (i, 0)),
        out_shape=jax.ShapeDtypeStruct((SIGMA * slots, NCELL), f32),
        compiler_params=PARAMS,
        name="interpolate",
    )(received.reshape(slots * 2 * SIGMA_PAD, 128), high, low)
    nest = nest.reshape(SIGMA, slots, NCELL).transpose(1, 0, 2)
    return (
        zonal_new,
        merid_new,
        tracer_new,
        nest.reshape(1, 1, slots, SIGMA, NCELL),
    )


def solution(mesh):
    return jax.shard_map(
        per_device,
        mesh=mesh,
        in_specs=(
            P(None, "lat", "lon"),
            P(None, "lat", "lon"),
            P(None, "lat", "lon"),
            P("lat", "lon"),
            P("lat", "lon", None),
            P("lat", "lon"),
        ),
        out_specs=(
            P(None, "lat", "lon"),
            P(None, "lat", "lon"),
            P(None, "lat", "lon"),
            P("lat", "lon", None, None, None),
        ),
        check_vma=False,
    )
```

```python
import functools
import math

import jax
import jax.numpy as jnp
import numpy as np
from jax import lax
from jax.experimental import pallas as pl
from jax.experimental.pallas import tpu as pltpu
from jax.sharding import PartitionSpec as P

SIGMA = 30
SIGMA_PAD = 32
TILE = 12
CAP = 2
BLK_X = 32
BLK_Y = 2
RIM = 256
NCELL = 1296
LEVEL_PAD = 80
CHUNK = 15

ADVECT = 0.25
DIFFUSE = 0.15
PRESSURE = 0.3
ROTATION = 0.6
BASE_LATITUDE = 20.0
ROW_DEGREES = 1.0 / 12.0

PARAMS = pltpu.CompilerParams(vmem_limit_bytes=48 * 2**20)


def cubic_weights(tile_cells):
    span_len = tile_cells + 4
    weights = np.zeros((span_len, 3 * tile_cells), np.float32)
    for cell_idx in range(tile_cells):
        for phase_idx in range(3):
            if phase_idx == 0:
                base_cell, fraction = (cell_idx - 1, 2.0 / 3.0)
            elif phase_idx == 1:
                base_cell, fraction = (cell_idx, 0.0)
            else:
                base_cell, fraction = (cell_idx, 1.0 / 3.0)
            coeffs = (
                (-(fraction**3) + 2 * fraction**2 - fraction) / 2,
                (3 * fraction**3 - 5 * fraction**2 + 2) / 2,
                (-3 * fraction**3 + 4 * fraction**2 + fraction) / 2,
                (fraction**3 - fraction**2) / 2,
            )
            for offset in range(4):
                weights[base_cell + 1 + offset, 3 * cell_idx + phase_idx] += coeffs[offset]
    return np.kron(weights, weights).astype(np.float32)


def coriolis_rows(row_index):
    degrees = BASE_LATITUDE + (row_index.astype(jnp.float32) + 0.5) * ROW_DEGREES
    latitude = degrees * (math.pi / 180.0)
    return (ROTATION * jnp.sin(latitude))[:, None]


def whole(shape):
    return pl.BlockSpec(shape, lambda i: (0,) * len(shape))


def pack_kernel(u_ref, v_ref, t_ref, first_row, last_row, first_col, last_col):
    step = pl.program_id(0)
    rows, cols = u_ref.shape[1:]
    lane = lax.broadcasted_iota(jnp.int32, (rows, 128), 1)

    @pl.when(step == 0)
    def _():
        first_row[...] = jnp.zeros_like(first_row)
        last_row[...] = jnp.zeros_like(last_row)
        first_col[...] = jnp.zeros_like(first_col)
        last_col[...] = jnp.zeros_like(last_col)

    for f, ref in enumerate((u_ref, v_ref, t_ref)):
        west = first_col[f]
        east = last_col[f]
        for i in range(CHUNK):
            k = step * CHUNK + i
            first_row[pl.ds(f * LEVEL_PAD + k, 1), :] = ref[i, 0:1, :]
            last_row[pl.ds(f * LEVEL_PAD + k, 1), :] = ref[i, rows - 1 : rows, :]
            here = lane == k
            west = jnp.where(here, ref[i, :, 0:128][:, 0:1], west)
            east = jnp.where(here, ref[i, :, cols - 128 : cols][:, 127:128], east)
        first_col[f] = west
        last_col[f] = east


def neighbours(x, f, k, east_ref, west_ref, north_ref, south_ref):
    rows, cols = x.shape
    col = lax.broadcasted_iota(jnp.int32, (rows, cols), 1)
    row = lax.broadcasted_iota(jnp.int32, (rows, cols), 0)
    e_col = pltpu.roll(east_ref[f], 127 - k, axis=1)[:, 127:128]
    w_col = pltpu.roll(west_ref[f], 127 - k, axis=1)[:, 127:128]
    n_row = north_ref[pl.ds(f * LEVEL_PAD + k, 1), :]
    s_row = south_ref[pl.ds(f * LEVEL_PAD + k, 1), :]
    east = jnp.where(col == cols - 1, e_col, pltpu.roll(x, cols - 1, axis=1))
    west = jnp.where(col == 0, w_col, pltpu.roll(x, 1, axis=1))
    north = jnp.where(row == rows - 1, n_row, pltpu.roll(x, rows - 1, axis=0))
    south = jnp.where(row == 0, s_row, pltpu.roll(x, 1, axis=0))
    return 0.5 * (east - west), 0.5 * (north - south), east + west + north + south - 4.0 * x


def tracer_kernel(
    u_ref, v_ref, t_ref, mask_ref, east_ref, west_ref, north_ref, south_ref,
    out_ref, tiles, low_rows, high_rows, west_cols, east_cols,
):
    step = pl.program_id(0)
    rows, cols = u_ref.shape[1:]
    sea = mask_ref[...].astype(jnp.float32)
    for i in range(CHUNK):
        k = step * CHUNK + i
        t = t_ref[i]
        gx, gy, lap = neighbours(t, 2, k, east_ref, west_ref, north_ref, south_ref)
        advect = u_ref[i] * gx + v_ref[i] * gy
        new = sea * (t - ADVECT * advect + DIFFUSE * lap)
        out_ref[i] = new
        for c in range(cols // 128):
            tiles[c, pl.ds(pl.multiple_of(k * rows, 8), rows), :] = new[:, c * 128 : c * 128 + 128]

    @pl.when(step == pl.num_programs(0) - 1)
    def _():
        count = tiles.shape[1] // rows
        lane = lax.broadcasted_iota(jnp.int32, (count, 128), 1)
        low_rows[...] = jnp.zeros_like(low_rows)
        high_rows[...] = jnp.zeros_like(high_rows)
        west_cols[...] = jnp.zeros_like(west_cols)
        east_cols[...] = jnp.zeros_like(east_cols)
        for r in range(2):
            for c in range(0, cols, 128):
                low_rows[r * LEVEL_PAD : r * LEVEL_PAD + count, c : c + 128] = tiles[
                    c // 128, pl.ds(r, count, stride=rows), :
                ]
                high_rows[r * LEVEL_PAD : r * LEVEL_PAD + count, c : c + 128] = tiles[
                    c // 128, pl.ds(rows - 2 + r, count, stride=rows), :
                ]
        west = jnp.zeros((count, 128), jnp.float32)
        east = jnp.zeros((count, 128), jnp.float32)
        for r in range(rows):
            here = (lane >= 2 * r) & (lane < 2 * r + 2)
            w = tiles[0, pl.ds(r, count, stride=rows), :]
            e = tiles[cols // 128 - 1, pl.ds(r, count, stride=rows), :]
            west = jnp.where(here, pltpu.roll(w, 2 * r, axis=1) if r else w, west)
            east = jnp.where(here, pltpu.roll(e, 2 * r + 2, axis=1), east)
        west_cols[0:count, :] = west
        east_cols[0:count, :] = east


def momentum_kernel(
    u_ref, v_ref, t_ref, mask_ref, coriolis_ref, east_ref, west_ref, north_ref, south_ref,
    zonal_ref, merid_ref,
):
    step = pl.program_id(0)
    sea = mask_ref[...].astype(jnp.float32)
    coriolis = coriolis_ref[...]
    halos = (east_ref, west_ref, north_ref, south_ref)
    for i in range(CHUNK):
        k = step * CHUNK + i
        u, v = u_ref[i], v_ref[i]
        t_gx, t_gy, _ = neighbours(t_ref[i], 2, k, *halos)
        gx, gy, lap = neighbours(u, 0, k, *halos)
        zonal_ref[i] = sea * (
            u - ADVECT * (u * gx + v * gy) + coriolis * v - PRESSURE * t_gx + DIFFUSE * lap
        )
        gx, gy, lap = neighbours(v, 1, k, *halos)
        merid_ref[i] = sea * (
            v - ADVECT * (u * gx + v * gy) - coriolis * u - PRESSURE * t_gy + DIFFUSE * lap
        )


def rim_kernel(
    block_ref, x_ref, east_ref, west_ref, north_ref, south_ref, inside_ref,
    out_ref, wide, rim,
):
    levels = inside_ref.shape[2]
    cols = x_ref.shape[0] * 128
    rows = x_ref.shape[1] // levels
    lane = lax.broadcasted_iota(jnp.int32, (levels, 128), 1)

    def side(east, west, r):
        e = pltpu.roll(east, 128 - 2 * r, axis=1) if r else east
        w = pltpu.roll(west, 126 - 2 * r, axis=1)
        return jnp.where(lane < 64, e, w)

    for r in range(rows):
        for c in range(0, cols, 128):
            wide[r + 2, 0:levels, c : c + 128] = x_ref[c // 128, pl.ds(r, levels, stride=rows), :]
        wide[r + 2, 0:levels, cols : cols + 128] = side(
            east_ref[0:levels, :], west_ref[0:levels, :], r
        )
    second_set = slice(LEVEL_PAD, LEVEL_PAD + levels)
    for j in range(2):
        at = slice(j * LEVEL_PAD, j * LEVEL_PAD + levels)
        wide[j, 0:levels, 0:cols] = south_ref[at, 0:cols]
        wide[j, 0:levels, cols : cols + 128] = side(
            south_ref[0:levels, cols:], south_ref[second_set, cols:], rows - 2 + j
        )
        wide[rows + 2 + j, 0:levels, 0:cols] = north_ref[at, 0:cols]
        wide[rows + 2 + j, 0:levels, cols : cols + 128] = side(
            north_ref[0:levels, cols:], north_ref[second_set, cols:], j
        )

    ring = cols + 128

    def slot(s, carry):
        b = block_ref[s]
        by, bx = b // BLK_X, b % BLK_X
        start = (TILE * bx - 2 + ring) % ring
        first, off = start // 128, start % 128
        second = (first + 1) % (ring // 128)
        first = pl.multiple_of(first * 128, 128)
        second = pl.multiple_of(second * 128, 128)
        for half in range(2):
            acc = jnp.zeros((levels, 128), jnp.float32)
            for q in range(8):
                r = by * TILE + half * 8 + q
                a = wide[r, 0:levels, pl.ds(first, 128)]
                z = wide[r, 0:levels, pl.ds(second, 128)]
                both = jnp.where(lane >= off, a, z)
                both = pltpu.roll(both, (16 * q - off + 128) % 128, axis=1)
                acc = jnp.where((lane >= 16 * q) & (lane < 16 * q + 16), both, acc)
            rim[0:levels, half * 128 : half * 128 + 128] = acc
        inside = inside_ref[s]
        x = rim[0:levels, :]
        high = x.astype(jnp.bfloat16)
        low = (x - high.astype(jnp.float32)).astype(jnp.bfloat16)
        ones = inside.astype(jnp.bfloat16)
        total = jnp.dot(ones, high, preferred_element_type=jnp.float32) + jnp.dot(
            ones, low, preferred_element_type=jnp.float32
        )
        count = jnp.sum(inside, axis=1, keepdims=True)
        total = total / jnp.maximum(count, 1.0)
        out_ref[s, 0] = total[:, 0:128]
        out_ref[s, 1] = total[:, 128:256]
        return carry

    lax.fori_loop(0, out_ref.shape[0], slot, 0)


def interp_kernel(x_ref, high_ref, low_ref, out_ref):
    slots = x_ref.shape[0] // (2 * SIGMA_PAD)
    per_step = out_ref.shape[0] // slots
    step = pl.program_id(0)
    for i in range(per_step):
        s = step * per_step + i
        halves = [
            x_ref[pl.ds(h * SIGMA_PAD + s, slots, stride=2 * SIGMA_PAD), :] for h in range(2)
        ]
        x = jnp.concatenate(halves, axis=1)
        high = x.astype(jnp.bfloat16)
        low = (x - high.astype(jnp.float32)).astype(jnp.bfloat16)
        both = jnp.concatenate([high, low], axis=0)
        wide = jnp.dot(both, high_ref[...], preferred_element_type=jnp.float32)
        out_ref[i * slots : (i + 1) * slots, :] = (
            wide[:slots]
            + wide[slots:]
            + jnp.dot(high, low_ref[...], preferred_element_type=jnp.float32)
        )


def shift(x, axis, wrap, forward):
    count = lax.axis_size(axis)
    up = [(i, (i + 1) % count) for i in range(count if wrap else count - 1)]
    return lax.ppermute(x, axis, up if forward else [(j, i) for i, j in up])


def per_device(zonal_velocity, meridional_velocity, tracer, land_mask, remap_bounds, nest_owner):
    levels, rows, cols = tracer.shape
    lon_count = lax.axis_size("lon")
    slots = CAP * lon_count
    steps = levels // CHUNK
    f32 = jnp.float32
    fields = (zonal_velocity, meridional_velocity, tracer)
    field_spec = pl.BlockSpec((CHUNK, rows, cols), lambda i: (i, 0, 0))
    row_shape, col_shape = (3 * LEVEL_PAD, cols), (3, rows, 128)
    field_bytes = levels * rows * cols * 4

    first_row, last_row, first_col, last_col = pl.pallas_call(
        pack_kernel,
        grid=(steps,),
        in_specs=[field_spec] * 3,
        out_specs=[whole(row_shape)] * 2 + [whole(col_shape)] * 2,
        out_shape=[jax.ShapeDtypeStruct(row_shape, f32)] * 2
        + [jax.ShapeDtypeStruct(col_shape, f32)] * 2,
        compiler_params=PARAMS,
        name="pack_edges",
    )(*fields)
    north = shift(first_row, "lat", False, False)
    south = shift(last_row, "lat", False, True)
    east = shift(first_col, "lon", True, False)
    west = shift(last_col, "lon", True, True)
    halos = (east, west, north, south)
    halo_specs = [whole(col_shape)] * 2 + [whole(row_shape)] * 2

    margin_row, margin_col = (2 * LEVEL_PAD, cols), (LEVEL_PAD, 128)
    tile_shape = (cols // 128, levels * rows, 128)
    tracer_new, tiles, low_rows, high_rows, west_cols, east_cols = pl.pallas_call(
        tracer_kernel,
        grid=(steps,),
        in_specs=[field_spec] * 3 + [whole((rows, cols))] + halo_specs,
        out_specs=[field_spec, whole(tile_shape)] + [whole(margin_row)] * 2 + [whole(margin_col)] * 2,
        out_shape=[jax.ShapeDtypeStruct(s, f32) for s in (tracer.shape, tile_shape)]
        + [jax.ShapeDtypeStruct(margin_row, f32)] * 2
        + [jax.ShapeDtypeStruct(margin_col, f32)] * 2,
        compiler_params=PARAMS,
        name="tracer_step",
    )(*fields, land_mask, *halos)
    east_margin = shift(west_cols, "lon", True, False)
    west_margin = shift(east_cols, "lon", True, True)
    sides = jnp.concatenate([east_margin, west_margin], axis=0)
    north_margin = shift(jnp.concatenate([low_rows, sides], axis=1), "lat", False, False)
    south_margin = shift(jnp.concatenate([high_rows, sides], axis=1), "lat", False, True)

    row_index = lax.axis_index("lat") * rows + jnp.arange(rows, dtype=jnp.int32)
    coriolis = jnp.broadcast_to(coriolis_rows(row_index), (rows, cols))
    zonal_new, merid_new = pl.pallas_call(
        momentum_kernel,
        grid=(steps,),
        in_specs=[field_spec] * 3 + [whole((rows, cols))] * 2 + halo_specs,
        out_specs=[field_spec] * 2,
        out_shape=[jax.ShapeDtypeStruct(tracer.shape, f32)] * 2,
        compiler_params=PARAMS,
        cost_estimate=pl.CostEstimate(
            flops=60 * levels * rows * cols, bytes_accessed=5 * field_bytes, transcendentals=0
        ),
        name="momentum_step",
    )(*fields, land_mask, coriolis, *halos)

    per_dev = BLK_Y * BLK_X
    owners = nest_owner.reshape(per_dev)
    bounds = remap_bounds.reshape(per_dev, SIGMA + 1)
    number = jnp.arange(per_dev, dtype=jnp.int32)
    earlier = (owners[None, :] == owners[:, None]) & (number[None, :] < number[:, None])
    rank_of = jnp.sum(earlier.astype(jnp.int32), axis=1)
    target = jnp.where(owners < lon_count, owners * CAP + rank_of, slots)
    chosen = (target[None, :] == jnp.arange(slots, dtype=jnp.int32)[:, None]).astype(jnp.int32)
    block_of = jnp.sum(chosen * number[None, :], axis=1)
    edges = jnp.sum(chosen[:, :, None] * bounds[None], axis=1)
    edges = jnp.pad(edges, ((0, 0), (0, SIGMA_PAD - SIGMA)), mode="edge")
    level = jnp.arange(levels, dtype=jnp.int32)[None, None, :]
    inside = ((level >= edges[:, :-1, None]) & (level < edges[:, 1:, None])).astype(f32)

    vmem = pl.BlockSpec(memory_space=pltpu.VMEM)
    sigma_blocks = pl.pallas_call(
        rim_kernel,
        in_specs=[pl.BlockSpec(memory_space=pltpu.SMEM)] + [vmem] * 6,
        out_specs=vmem,
        out_shape=jax.ShapeDtypeStruct((slots, 2, SIGMA_PAD, 128), f32),
        scratch_shapes=[
            pltpu.VMEM((rows + 4, LEVEL_PAD, cols + 128), f32),
            pltpu.VMEM((LEVEL_PAD, RIM), f32),
        ],
        compiler_params=PARAMS,
        name="sigma_rims",
    )(
        block_of, tiles, east_margin, west_margin, north_margin, south_margin,
        jnp.pad(inside, ((0, 0), (0, SIGMA_PAD - inside.shape[1]), (0, 0))),
    )
    received = lax.all_to_all(
        sigma_blocks.reshape(lon_count, CAP * 2 * SIGMA_PAD, 128),
        "lon", split_axis=0, concat_axis=0, tiled=True,
    )

    table = cubic_weights(TILE)
    high = jnp.asarray(table).astype(jnp.bfloat16)
    low = (jnp.asarray(table) - high.astype(f32)).astype(jnp.bfloat16)
    per_step = 6
    nest = pl.pallas_call(
        interp_kernel,
        grid=(SIGMA // per_step,),
        in_specs=[whole((slots * 2 * SIGMA_PAD, 128))] + [whole((RIM, NCELL))] * 2,
        out_specs=pl.BlockSpec((per_step * slots, NCELL), lambda i: (i, 0)),
        out_shape=jax.ShapeDtypeStruct((SIGMA * slots, NCELL), f32),
        compiler_params=PARAMS,
        name="interpolate",
    )(received.reshape(slots * 2 * SIGMA_PAD, 128), high, low)
    nest = nest.reshape(SIGMA, slots, NCELL).transpose(1, 0, 2)
    return (
        zonal_new,
        merid_new,
        tracer_new,
        nest.reshape(1, 1, slots, SIGMA, NCELL),
    )


def solution(mesh):
    return jax.shard_map(
        per_device,
        mesh=mesh,
        in_specs=(
            P(None, "lat", "lon"),
            P(None, "lat", "lon"),
            P(None, "lat", "lon"),
            P("lat", "lon"),
            P("lat", "lon", None),
            P("lat", "lon"),
        ),
        out_specs=(
            P(None, "lat", "lon"),
            P(None, "lat", "lon"),
            P(None, "lat", "lon"),
            P("lat", "lon", None, None, None),
        ),
        check_vma=False,
    )
```
